256 devices in a mesh: scen: 8 (over z_lo, y), obl: 32 (over z_hi, x, core).
Axes of the slice: x: 4, y: 4, z: 8 (z_hi: 4, z_lo: 2; z = z_hi * 2 + z_lo), core: 2. Of those that a mesh axis runs over, the one named last changes fastest.
Arguments:
- factor_draws: bfloat16 [16384, 128], P(('scen', 'obl')), may hold values from -5 to 5
- loadings: bfloat16 [131072, 128], P(('scen', 'obl')), may hold values from -0.45 to 0.5
- sector: int32 [131072], P(('scen', 'obl')), may hold values from 0 to 11
- threshold: bfloat16 [131072], P(('scen', 'obl')), may hold values from -3.59375 to -2.796875
- idio: bfloat16 [131072], P(('scen', 'obl')), may hold values from 0.59765625 to 1
- exposure: bfloat16 [131072], P(('scen', 'obl')), may hold values from 0.19921875 to 1
- theta: float32 [1], replicated, may hold values from 1 to 2
Outputs:
- relative_weights: float32 [16384], P(('scen', 'obl'))
- sensitivities: float32 [131072, 128], P(('scen', 'obl'))
The draws below stay inside these ranges and needn't reach their ends.
All inputs are finite; a program needn't handle non-finite values.
Results may differ from the reference program's by a relative error of at most 0.0035.
Values may be sent and summed in bfloat16 or wider, within the bound.
A program may use at most 64 MiB of HBM per device.

```python
import math
import jax
import jax.numpy as jnp
from jax import lax

FACTORS = 128
GLOBAL_F = 32
SECTORS = 12
SECTOR_F = 8
OBLIGORS = 131072
SCENARIOS = 16384


def draw_loadings(key, part):
    key = jax.random.fold_in(key, 11)
    width = min(0.14, 0.024)
    noise = jax.random.normal(key, (OBLIGORS, FACTORS), jnp.float32)
    values = width * jnp.clip(noise, -3.0, 3.0)
    return values.astype(jnp.bfloat16)


def with_ends(array, key, least, high):
    spot = [jax.random.randint(jax.random.fold_in(key, axis), (), 0, length) for axis, length in enumerate(array.shape)]
    longest = array.shape.index(max(array.shape))
    beside = spot[:longest] + [(spot[longest] + 1) % array.shape[longest]] + spot[longest + 1:]
    return array.at[tuple(spot)].set(least).at[tuple(beside)].set(high)


def level_of(rng, dims, split, low, high):
    def one(axis_at, shards_of):
        steps = jax.random.uniform(jax.random.fold_in(jax.random.fold_in(rng, 6), axis_at), (shards_of,), jnp.float32, low / len(split), high / len(split))
        return jnp.repeat(jnp.exp(steps), dims[axis_at] // shards_of).reshape((-1,) + (1,) * (len(dims) - axis_at - 1))

    factor_of = one(*split[0])
    for cut in split[1:]:
        factor_of = factor_of * one(*cut)
    return factor_of


def normal_values(stream_key, dims, deviation, reach, split=(), dtype=jnp.bfloat16):
    entries = jax.random.normal(stream_key, dims, jnp.float32) * deviation
    if len(split) > 0:
        entries = level_of(stream_key, dims, split, -0.22, 0.18) * entries
    return jnp.clip(entries, min=-reach, max=reach).astype(dtype)


def setup_inputs(seed: int = 0) -> dict:
    arg_keys = jax.random.split(jax.random.key(seed), 8)
    factor_draws = normal_values(arg_keys[0], (SCENARIOS, FACTORS), 1.0, 5.0, ((0, 256),))
    loadings = draw_loadings(jax.random.fold_in(arg_keys[7], 71), 0)
    sector = with_ends(jax.random.randint(arg_keys[2], (OBLIGORS,), 0, SECTORS), jax.random.fold_in(arg_keys[2], 1), 0, SECTORS - 1).astype(jnp.int32)
    threshold = jnp.clip(-3.59375 + 0.796875 * jax.random.uniform(arg_keys[3], (OBLIGORS,), jnp.float32) ** level_of(arg_keys[3], (OBLIGORS,), ((0, 256),), -0.2, 0.2), -3.59375, -2.796875).astype(jnp.bfloat16)
    idio = jnp.clip(0.59765625 + 0.40234375 * jax.random.uniform(arg_keys[4], (OBLIGORS,), jnp.float32) ** level_of(arg_keys[4], (OBLIGORS,), ((0, 256),), -0.2, 0.2), 0.59765625, 1.0).astype(jnp.bfloat16)
    exposure = jnp.clip(jnp.exp(math.log(1.0) - 1.6133518 * jax.random.uniform(arg_keys[5], (OBLIGORS,), jnp.float32) ** level_of(arg_keys[5], (OBLIGORS,), ((0, 256),), -0.2, 0.2)), 0.19921875, 1.0).astype(jnp.bfloat16)
    theta = jnp.clip(jax.random.uniform(arg_keys[6], (1,), jnp.float32, 1.0, 2.0), 1.0, 2.0)
    return dict(factor_draws=factor_draws, loadings=loadings, sector=sector, threshold=threshold, idio=idio, exposure=exposure, theta=theta)


ROOT_HALF = 0.7071067811865476
NORMAL_PEAK = 0.3989422804014327
SCALE_OUT = 300.0


def sector_mask(sector):
    column_ids = lax.broadcasted_iota(jnp.int32, (sector.shape[0], FACTORS), 1)
    in_block = (column_ids - GLOBAL_F) // SECTOR_F == sector[:, None]
    return (column_ids < GLOBAL_F) | in_block


def obligor_terms(scores, limits, spreads, amounts, twist):
    shifted = (limits[None, :] + scores) / spreads[None, :]
    prob = 0.5 * jax.scipy.special.erfc(-shifted * ROOT_HALF)
    growth = jnp.exp(twist * amounts)[None, :]
    denom = 1.0 + prob * (growth - 1.0)
    twisted = prob * growth / denom
    return shifted, growth, denom, twisted


def reference(factor_draws, loadings, sector, threshold, idio, exposure, theta):
    twist = theta[0]
    mask = sector_mask(sector)
    active = jnp.where(mask, loadings, jnp.zeros_like(loadings))
    block = math.gcd(OBLIGORS, 4096)
    count = OBLIGORS // block
    pieces = (active.reshape(count, block, FACTORS),
              threshold.astype(jnp.float32).reshape(count, block),
              idio.astype(jnp.float32).reshape(count, block),
              exposure.astype(jnp.float32).reshape(count, block))

    def first(piece):
        block_rows, limits, spreads, amounts = piece
        scores = jnp.dot(factor_draws, block_rows.T, preferred_element_type=jnp.float32)
        shifted, growth, denom, twisted = obligor_terms(scores, limits, spreads, amounts, twist)
        return jnp.sum(jnp.log(denom) - twist * amounts[None, :] * twisted, axis=1)

    logit = jnp.sum(lax.map(first, pieces), axis=0)
    top = jnp.max(logit)
    unnormed = jnp.exp(logit - top)
    weights = unnormed / jnp.sum(unnormed)

    def second(piece):
        block_rows, limits, spreads, amounts = piece
        scores = jnp.dot(factor_draws, block_rows.T, preferred_element_type=jnp.float32)
        shifted, growth, denom, twisted = obligor_terms(scores, limits, spreads, amounts, twist)
        slope = (SCALE_OUT * weights[:, None] * amounts[None, :] * growth / (denom * denom)
                 * NORMAL_PEAK * jnp.exp(-0.5 * shifted * shifted) / spreads[None, :]).astype(jnp.bfloat16)
        return jnp.dot(slope.T, factor_draws, preferred_element_type=jnp.float32)

    sensitivity = lax.map(second, pieces).reshape(OBLIGORS, FACTORS)
    return SCENARIOS * weights, jnp.where(mask, sensitivity, 0.0)
```

```python
import functools

import jax
import jax.numpy as jnp
from jax import lax
from jax.experimental import pallas as pl
from jax.experimental.pallas import tpu as pltpu
from jax.sharding import PartitionSpec as P

F32 = jnp.float32
BF16 = jnp.bfloat16
MESH = pl.DeviceIdType.MESH
LANES = 128
FACTORS = 128
GLOBAL_F = 32
SECTOR_F = 8
SIDE = 4
DEPTH = 8
OWN = 64
UNIT = DEPTH * OWN
HALF = SIDE * SIDE * UNIT
SCENARIOS = 2 * HALF
UNITS = SCENARIOS // UNIT
OBL = 512
ROWS = 128
GROUP = 64
STRETCH = 256
PEERS = SIDE * SIDE
ROOT_HALF = 0.7071067811865476
NORMAL_PEAK = 0.3989422804014327
SCALE_OUT = 300.0
LOG2_E = 1.4426950408889634
NT = (((1,), (1,)), ((), ()))


def place():
    scen, obl = lax.axis_index("scen"), lax.axis_index("obl")
    z = (obl // 8) * 2 + scen // 4
    return (obl // 2) % 4, scen % 4, z, obl % 2


def device(x, y, z, core):
    return ((z % 2) * 4 + y, (z // 2) * 8 + x * 2 + core)


def columns(row):
    return jnp.transpose(jnp.broadcast_to(row, (LANES, LANES)))


def wide(value):
    return jnp.concatenate([value] * (UNIT // LANES), axis=1)


def kernel(
    draws_ref,
    load_ref,
    sector_ref,
    threshold_ref,
    idio_ref,
    exposure_ref,
    theta_ref,
    weight_ref,
    sens_ref,
    draws,
    slopes,
    active,
    inverse,
    offset,
    shift,
    gain,
    centre,
    level,
    scale,
    logit,
    total,
    part1,
    part2,
    send1,
    recv1,
    send2,
    recv2,
    send3,
    recv3,
    send_f,
    recv_f,
    send_r,
    recv_r,
):
    x, y, z, core = place()
    p1 = y + core * (x - y)
    p2 = x + core * (y - x)

    def along1(step):
        q = (p1 + step) % SIDE
        return device(x + core * (q - x), y + (1 - core) * (q - y), z, core)

    def along2(step):
        q = (p2 + step) % SIDE
        return device(x + (1 - core) * (q - x), y + core * (q - y), z, core)

    partner = device(x, y, z, 1 - core)
    plane = x * SIDE + y
    stack = z * 2 + core

    def plane_peer(j):
        return device(j // SIDE, j % SIDE, z, core)

    def stack_peer(j):
        return device(x, y, j // 2, j % 2)

    barrier = pltpu.get_barrier_semaphore()
    for step in range(1, PEERS):
        for peer in (plane_peer((plane + step) % PEERS), stack_peer((stack + step) % PEERS)):
            pl.semaphore_signal(barrier, inc=1, device_id=peer, device_id_type=MESH)
    pl.semaphore_wait(barrier, 2 * (PEERS - 1))

    def unit_index(half, a, b):
        return half * PEERS + a * SIDE + b

    def unit_rows(index):
        return pl.ds(pl.multiple_of(index * UNIT, UNIT), UNIT)

    def own_index(d, e):
        return unit_index(core, (p2 + SIDE - d) % SIDE, (p1 + SIDE - e) % SIDE)

    def partner_index(d, e):
        return unit_index(1 - core, (p1 + SIDE - d) % SIDE, (p2 + SIDE - e) % SIDE)

    def copy1(step, from_z):
        rows = pl.ds(pl.multiple_of(own_index(0, 0) * UNIT + from_z * OWN, OWN), OWN)
        return pltpu.make_async_remote_copy(
            src_ref=draws_ref,
            dst_ref=draws.at[rows],
            send_sem=send1.at[step],
            recv_sem=recv1.at[step],
            device_id=device(x, y, (z + step) % DEPTH, core),
            device_id_type=MESH,
        )

    def unit_copy(index, send, recv, peer):
        rows = unit_rows(index)
        return pltpu.make_async_remote_copy(
            src_ref=draws.at[rows],
            dst_ref=draws.at[rows],
            send_sem=send,
            recv_sem=recv,
            device_id=peer,
            device_id_type=MESH,
        )

    def copy2(step, e):
        return unit_copy(own_index(0, e), send2.at[step], recv2.at[step], along1(step))

    def copy3(e, step, d):
        return unit_copy(own_index(d, e), send3.at[e, step], recv3.at[e, step], along2(step))

    def forward(d, e, index):
        return unit_copy(index, send_f.at[d, e], recv_f.at[d, e], partner)

    for step in range(1, DEPTH):
        copy1(step, z).start()
    mine = pl.ds(pl.multiple_of(own_index(0, 0) * UNIT + z * OWN, OWN), OWN)
    draws[mine, :] = draws_ref[...]

    twist = theta_ref[0]
    ids = lax.broadcasted_iota(jnp.int32, (LANES, FACTORS), 1)
    for block in range(OBL // LANES):
        rows = pl.ds(block * LANES, LANES)
        one = pl.ds(block, 1)
        idio = idio_ref[one, :].astype(F32)
        amount = exposure_ref[one, :].astype(F32)
        limit = threshold_ref[one, :].astype(F32)
        growth = jnp.exp(twist * amount)
        half = 0.5 * (growth - 1.0)
        spread = ROOT_HALF / idio
        costs = twist * amount * growth / (growth - 1.0)
        inverse[rows, :] = columns(spread)
        offset[rows, :] = columns(limit * spread)
        shift[rows, :] = columns(1.0 / half + 1.0)
        gain[rows, :] = columns(costs / half)
        scale[rows, :] = columns(
            (SCALE_OUT * NORMAL_PEAK) * amount * growth / (idio * half * half)
        )
        full_cost = columns(costs)
        for group in range(LANES // GROUP):
            part = full_cost[group * GROUP : (group + 1) * GROUP]
            centre[pl.ds((block * LANES // GROUP + group) * 8, 8), :] = jnp.sum(
                part.reshape(GROUP // 8, 8, LANES), axis=0
            )
        full_half = columns(half).reshape(LANES // 8, 8, LANES)
        product = full_half[0]
        for k in range(1, LANES // 8):
            product = product * full_half[k]
        at = pl.ds((block * LANES // STRETCH) * 8, 8)
        if (block * LANES) % STRETCH == 0:
            level[at, :] = product
        else:
            level[at, :] = level[at, :] * product
        sector = columns(sector_ref[one, :].astype(F32)).astype(jnp.int32)
        first = GLOBAL_F + sector * SECTOR_F
        mask = (ids < GLOBAL_F) | ((ids >= first) & (ids < first + SECTOR_F))
        active[rows, :] = jnp.where(mask, load_ref[rows, :].astype(F32), 0.0).astype(BF16)
        scale[rows, :] = jnp.where(mask, scale[rows, :], 0.0)

    def compute(index):
        draw_rows = draws[unit_rows(index), :]
        lanes = pl.ds(pl.multiple_of(index * UNIT, UNIT), UNIT)
        acc = jnp.zeros((8, UNIT), F32)
        product = None
        for r in range(0, OBL, ROWS):
            rows = pl.ds(r, ROWS)
            score = lax.dot_general(active[rows, :], draw_rows, NT, preferred_element_type=F32)
            arg = score * wide(inverse[rows, :]) + wide(offset[rows, :])
            denom = lax.erf(arg) + wide(shift[rows, :])
            share = pl.reciprocal(denom)
            slopes[rows, lanes] = (jnp.exp2((arg * arg) * -LOG2_E) * share * share).astype(BF16)
            loss = share * wide(gain[rows, :])
            if r % STRETCH == 0:
                product = denom[:8]
            for k in range(0 if r % STRETCH else 1, ROWS // 8):
                product = product * denom[k * 8 : k * 8 + 8]
            for g in range(0, ROWS, GROUP):
                some = loss[g : g + 8]
                for k in range(1, GROUP // 8):
                    some = some + loss[g + k * 8 : g + k * 8 + 8]
                acc = acc + (some - wide(centre[pl.ds((r + g) // GROUP * 8, 8), :]))
            if (r + ROWS) % STRETCH == 0:
                acc = acc + jnp.log(product * wide(level[pl.ds(r // STRETCH * 8, 8), :]))
        logit[pl.ds(index, 1), :] = jnp.sum(acc, axis=0, keepdims=True)

    for step in range(1, DEPTH):
        copy1(step, (z + DEPTH - step) % DEPTH).wait_recv()
    for step in range(1, SIDE):
        copy2(step, 0).start()

    def turn(n, carry):
        group, e = n // SIDE, n % SIDE
        d = group + (group // 2) * (5 - 2 * group)

        @pl.when((n > 0) & (n < SIDE))
        def _():
            copy2(e, e).wait_recv()

        @pl.when(n >= SIDE)
        def _():
            copy3(e, d, d).wait_recv()

        @pl.when(n < SIDE)
        def _():
            for step in range(1, SIDE):
                copy3(e, step, 0).start()

        forward(d, e, own_index(d, e)).start()

        def side(which, carry):
            @pl.when(which == 1)
            def _():
                forward(d, e, partner_index(d, e)).wait_recv()

            compute(own_index(d, e) + which * (partner_index(d, e) - own_index(d, e)))
            return carry

        return lax.fori_loop(0, 2, side, carry)

    lax.fori_loop(0, UNITS // 2, turn, 0)

    def tile(j):
        return (
            pl.ds(pl.multiple_of(j // SIDE * 8, 8), 8),
            pl.ds(pl.multiple_of(j % SIDE * LANES, LANES), LANES),
        )

    def reduce1(step, j, peer):
        return pltpu.make_async_remote_copy(
            src_ref=logit.at[tile(j)],
            dst_ref=part1.at[plane],
            send_sem=send_r.at[0, step],
            recv_sem=recv_r.at[0, step],
            device_id=peer,
            device_id_type=MESH,
        )

    def reduce2(step, peer):
        return pltpu.make_async_remote_copy(
            src_ref=part2.at[stack],
            dst_ref=part2.at[stack],
            send_sem=send_r.at[1, step],
            recv_sem=recv_r.at[1, step],
            device_id=peer,
            device_id_type=MESH,
        )

    def reduce3(step, peer):
        return pltpu.make_async_remote_copy(
            src_ref=total.at[tile(plane)],
            dst_ref=total.at[tile(plane)],
            send_sem=send_r.at[2, step],
            recv_sem=recv_r.at[2, step],
            device_id=peer,
            device_id_type=MESH,
        )

    def arrival1(step):
        j = (plane + PEERS - step) % PEERS
        return pltpu.make_async_remote_copy(
            src_ref=logit.at[tile(plane)],
            dst_ref=part1.at[j],
            send_sem=send_r.at[0, step],
            recv_sem=recv_r.at[0, step],
            device_id=plane_peer(j),
            device_id_type=MESH,
        )

    def arrival2(step):
        j = (stack + PEERS - step) % PEERS
        return pltpu.make_async_remote_copy(
            src_ref=part2.at[stack],
            dst_ref=part2.at[j],
            send_sem=send_r.at[1, step],
            recv_sem=recv_r.at[1, step],
            device_id=stack_peer(j),
            device_id_type=MESH,
        )

    def arrival3(step):
        j = (plane + PEERS - step) % PEERS
        return pltpu.make_async_remote_copy(
            src_ref=total.at[tile(plane)],
            dst_ref=total.at[tile(j)],
            send_sem=send_r.at[2, step],
            recv_sem=recv_r.at[2, step],
            device_id=plane_peer(j),
            device_id_type=MESH,
        )

    def to_plane(step):
        j = (plane + step) % PEERS
        return reduce1(step, j, plane_peer(j))

    def to_stack(step):
        return reduce2(step, stack_peer((stack + step) % PEERS))

    def back_to_plane(step):
        return reduce3(step, plane_peer((plane + step) % PEERS))

    for step in range(1, PEERS):
        to_plane(step).start()
    part1[plane] = logit[tile(plane)]
    for step in range(1, PEERS):
        arrival1(step).wait_recv()
    part2[stack] = jnp.sum(part1[...], axis=0)
    for step in range(1, PEERS):
        to_stack(step).start()
    for step in range(1, PEERS):
        arrival2(step).wait_recv()
    total[tile(plane)] = jnp.sum(part2[...], axis=0)
    for step in range(1, PEERS):
        back_to_plane(step).start()

    for step in range(1, DEPTH):
        copy1(step, z).wait_send()
    for step in range(1, SIDE):
        copy2(step, 0).wait_send()
        for e in range(SIDE):
            copy3(e, step, 0).wait_send()
    for d in range(SIDE):
        for e in range(SIDE):
            forward(d, e, own_index(d, e)).wait_send()
    for step in range(1, PEERS):
        to_plane(step).wait_send()
        to_stack(step).wait_send()
    for step in range(1, PEERS):
        arrival3(step).wait_recv()
    for step in range(1, PEERS):
        back_to_plane(step).wait_send()

    logits = total[...]
    raw = jnp.exp(logits - jnp.max(logits))
    norm = 1.0 / jnp.sum(raw)
    total[...] = raw
    own_row = total[pl.ds(own_index(0, 0), 1), :]
    own = jnp.zeros((1, OWN), F32)
    for k in range(DEPTH):
        own = jnp.where(z == k, own_row[:, k * OWN : (k + 1) * OWN], own)
    weight_ref[...] = own * (norm * SCENARIOS)

    for j in range(UNIT // LANES):
        turned = jnp.transpose(raw[:, j * LANES : (j + 1) * LANES])
        for u in range(UNITS):
            rows = pl.ds(u * UNIT + j * LANES, LANES)
            draws[rows, :] = (draws[rows, :].astype(F32) * turned[:, u : u + 1]).astype(BF16)

    sens_ref[...] = jnp.zeros_like(sens_ref)
    depth = 2 * UNIT

    def add(n, carry):
        at = pl.ds(pl.multiple_of(n * depth, depth), depth)
        sens_ref[...] += jnp.dot(slopes[:, at], draws[at, :], preferred_element_type=F32)
        return carry

    lax.fori_loop(0, SCENARIOS // depth, add, 0)
    sens_ref[...] = sens_ref[...] * (scale[...] * norm)


def shards(factor_draws, loadings, sector, threshold, idio, exposure, theta):
    rows = OBL // LANES
    vmem = pl.BlockSpec(memory_space=pltpu.VMEM)
    constant = pltpu.VMEM((OBL, LANES), F32)
    dma = pltpu.SemaphoreType.DMA
    weights, sensitivities = pl.pallas_call(
        kernel,
        out_shape=[
            jax.ShapeDtypeStruct((1, OWN), F32),
            jax.ShapeDtypeStruct((OBL, FACTORS), F32),
        ],
        in_specs=[vmem] * 6 + [pl.BlockSpec(memory_space=pltpu.SMEM)],
        out_specs=[vmem] * 2,
        scratch_shapes=[
            pltpu.VMEM((SCENARIOS, FACTORS), BF16),
            pltpu.VMEM((OBL, SCENARIOS), BF16),
            pltpu.VMEM((OBL, FACTORS), BF16),
            constant,
            constant,
            constant,
            constant,
            pltpu.VMEM((OBL // GROUP * 8, LANES), F32),
            pltpu.VMEM((OBL // STRETCH * 8, LANES), F32),
            constant,
            pltpu.VMEM((UNITS, UNIT), F32),
            pltpu.VMEM((UNITS, UNIT), F32),
            pltpu.VMEM((PEERS, 8, LANES), F32),
            pltpu.VMEM((PEERS, 8, LANES), F32),
            dma((DEPTH,)),
            dma((DEPTH,)),
            dma((SIDE,)),
            dma((SIDE,)),
            dma((SIDE, SIDE)),
            dma((SIDE, SIDE)),
            dma((SIDE, SIDE)),
            dma((SIDE, SIDE)),
            dma((3, PEERS)),
            dma((3, PEERS)),
        ],
        compiler_params=pltpu.CompilerParams(
            collective_id=0, has_side_effects=True, vmem_limit_bytes=56 << 20
        ),
    )(
        factor_draws,
        loadings,
        sector.reshape(rows, LANES),
        threshold.reshape(rows, LANES),
        idio.reshape(rows, LANES),
        exposure.reshape(rows, LANES),
        theta,
    )
    return weights.reshape(OWN), sensitivities


def solution(mesh):
    return jax.shard_map(
        shards,
        mesh=mesh,
        in_specs=(
            P(("scen", "obl"), None),
            P(("scen", "obl"), None),
            P(("scen", "obl")),
            P(("scen", "obl")),
            P(("scen", "obl")),
            P(("scen", "obl")),
            P(),
        ),
        out_specs=(P(("scen", "obl")), P(("scen", "obl"), None)),
        check_vma=False,
    )
```

```python
import functools

import jax
import jax.numpy as jnp
from jax import lax
from jax.experimental import pallas as pl
from jax.experimental.pallas import tpu as pltpu
from jax.sharding import PartitionSpec as P

F32 = jnp.float32
BF16 = jnp.bfloat16
MESH = pl.DeviceIdType.MESH
LANES = 128
FACTORS = 128
GLOBAL_F = 32
SECTOR_F = 8
SIDE = 4
DEPTH = 8
OWN = 64
UNIT = DEPTH * OWN
HALF = SIDE * SIDE * UNIT
SCENARIOS = 2 * HALF
UNITS = SCENARIOS // UNIT
OBL = 512
ROWS = 128
GROUP = 64
STRETCH = 256
DEEP = 2048
FULL = 8
LAST = 2
PEERS = SIDE * SIDE
FAR_PLANE = sorted(range(1, PEERS), key=lambda s: -min(s // SIDE, SIDE - s // SIDE) - min(s % SIDE, SIDE - s % SIDE))
FAR_STACK = sorted(range(1, PEERS), key=lambda s: -min(s // 2, DEPTH - s // 2))
ROOT_HALF = 0.7071067811865476
NORMAL_PEAK = 0.3989422804014327
SCALE_OUT = 300.0
LOG2_E = 1.4426950408889634
NT = (((1,), (1,)), ((), ()))


def div(a, b):
    return lax.div(a, jnp.int32(b))


def rem(a, b):
    return lax.rem(a, jnp.int32(b))


def place():
    scen, obl = lax.axis_index("scen"), lax.axis_index("obl")
    z = div(obl, 8) * 2 + div(scen, 4)
    return rem(div(obl, 2), 4), rem(scen, 4), z, rem(obl, 2)


def device(x, y, z, core):
    return (rem(z, 2) * 4 + y, div(z, 2) * 8 + x * 2 + core)


def columns(row):
    return jnp.transpose(jnp.broadcast_to(row, (LANES, LANES)))


def wide(value):
    return jnp.concatenate([value] * (UNIT // LANES), axis=1)


def kernel(
    draws_hbm,
    load_hbm,
    sector_hbm,
    threshold_hbm,
    idio_hbm,
    exposure_hbm,
    theta_ref,
    weight_ref,
    sens_ref,
    load_ref,
    sector_ref,
    threshold_ref,
    idio_ref,
    exposure_ref,
    local,
    draws,
    slopes,
    kept,
    active,
    inverse,
    offset,
    shift,
    gain,
    centre,
    level,
    scale,
    logit,
    total,
    part1,
    part2,
    send1,
    recv1,
    send2,
    recv2,
    send3,
    recv3,
    send_h,
    recv_h,
    send_f,
    recv_f,
    send_r,
    recv_r,
):
    x, y, z, core = place()
    p1 = y + core * (x - y)
    p2 = x + core * (y - x)

    def along1(step):
        q = rem(p1 + step, SIDE)
        return device(x + core * (q - x), y + (1 - core) * (q - y), z, core)

    def along2(step):
        q = rem(p2 + step, SIDE)
        return device(x + (1 - core) * (q - x), y + core * (q - y), z, core)

    partner = device(x, y, z, 1 - core)
    plane = x * SIDE + y
    stack = z * 2 + core

    def plane_to(step):
        return rem(x + step // SIDE, SIDE) * SIDE + rem(y + step % SIDE, SIDE)

    def plane_from(step):
        return plane_to((SIDE - step // SIDE) % SIDE * SIDE + (SIDE - step % SIDE) % SIDE)

    def stack_to(step):
        return rem(z + step // 2, DEPTH) * 2 + rem(core + step % 2, 2)

    def stack_from(step):
        return stack_to((DEPTH - step // 2) % DEPTH * 2 + step % 2)

    def plane_peer(j):
        return device(div(j, SIDE), rem(j, SIDE), z, core)

    def stack_peer(j):
        return device(x, y, div(j, 2), rem(j, 2))

    def fetch(source, target, slot):
        copy = pltpu.make_async_copy(source, target, local.at[slot])
        copy.start()
        return copy

    inputs = [
        fetch(sector_hbm, sector_ref, 0),
        fetch(threshold_hbm, threshold_ref, 1),
        fetch(idio_hbm, idio_ref, 2),
        fetch(exposure_hbm, exposure_ref, 3),
        fetch(load_hbm, load_ref, 4),
    ]

    barrier = pltpu.get_barrier_semaphore()
    for step in range(1, PEERS):
        for peer in (plane_peer(plane_to(step)), stack_peer(stack_to(step))):
            pl.semaphore_signal(barrier, inc=1, device_id=peer, device_id_type=MESH)

    def unit_index(half, a, b):
        return half * PEERS + a * SIDE + b

    def unit_rows(index):
        return pl.ds(pl.multiple_of(index * UNIT, UNIT), UNIT)

    def own_index(d, e):
        return unit_index(core, rem(p2 + SIDE - d, SIDE), rem(p1 + SIDE - e, SIDE))

    def partner_index(d, e):
        return unit_index(1 - core, rem(p1 + SIDE - d, SIDE), rem(p2 + SIDE - e, SIDE))

    def copy1(step, from_z):
        rows = pl.ds(pl.multiple_of(own_index(0, 0) * UNIT + from_z * OWN, OWN), OWN)
        return pltpu.make_async_remote_copy(
            src_ref=draws.at[rows],
            dst_ref=draws.at[rows],
            send_sem=send1.at[step],
            recv_sem=recv1.at[step],
            device_id=device(x, y, rem(z + step, DEPTH), core),
            device_id_type=MESH,
        )

    def unit_copy(index, send, recv, peer):
        rows = unit_rows(index)
        return pltpu.make_async_remote_copy(
            src_ref=draws.at[rows],
            dst_ref=draws.at[rows],
            send_sem=send,
            recv_sem=recv,
            device_id=peer,
            device_id_type=MESH,
        )

    def copy2(step, e):
        return unit_copy(own_index(0, e), send2.at[step], recv2.at[step], along1(step))

    def copy3(e, step, d):
        return unit_copy(own_index(d, e), send3.at[e, step], recv3.at[e, step], along2(step))

    def relay(e, half):
        d, step = 1 + 2 * half, 1 + 2 * half
        rows = pl.ds(pl.multiple_of(own_index(d, e) * UNIT + half * (UNIT // 2), UNIT // 2), UNIT // 2)
        return relay_copy(rows, e, half, along2(step))

    def relayed(e, half):
        rows = pl.ds(pl.multiple_of(own_index(2, e) * UNIT + half * (UNIT // 2), UNIT // 2), UNIT // 2)
        return relay_copy(rows, e, half, along2(1 + 2 * half))

    def relay_copy(rows, e, half, peer):
        return pltpu.make_async_remote_copy(
            src_ref=draws.at[rows],
            dst_ref=draws.at[rows],
            send_sem=send_h.at[e, half],
            recv_sem=recv_h.at[e, half],
            device_id=peer,
            device_id_type=MESH,
        )

    def forward(d, e, index):
        return unit_copy(index, send_f.at[d, e], recv_f.at[d, e], partner)

    mine = pl.ds(pl.multiple_of(own_index(0, 0) * UNIT + z * OWN, OWN), OWN)
    own_draws = fetch(draws_hbm, draws.at[mine], 5)
    own_draws.wait()
    pl.semaphore_wait(barrier, 2 * (PEERS - 1))
    for step in (4, 3, 5, 2, 6, 1, 7):
        copy1(step, z).start()

    for copy in inputs:
        copy.wait()

    twist = theta_ref[0]
    ids = lax.broadcasted_iota(jnp.int32, (LANES, FACTORS), 1)
    for block in range(OBL // LANES):
        rows = pl.ds(block * LANES, LANES)
        one = pl.ds(block, 1)
        idio = idio_ref[one, :].astype(F32)
        amount = exposure_ref[one, :].astype(F32)
        limit = threshold_ref[one, :].astype(F32)
        growth = jnp.exp(twist * amount)
        half = 0.5 * (growth - 1.0)
        spread = ROOT_HALF / idio
        costs = twist * amount * growth / (growth - 1.0)
        inverse[rows, :] = columns(spread)
        offset[rows, :] = columns(limit * spread)
        shift[rows, :] = columns(1.0 / half + 1.0)
        gain[rows, :] = columns(costs / half)
        scale[rows, :] = columns(
            (SCALE_OUT * NORMAL_PEAK) * amount * growth / (idio * half * half)
        )
        full_cost = columns(costs)
        for group in range(LANES // GROUP):
            part = full_cost[group * GROUP : (group + 1) * GROUP]
            centre[pl.ds((block * LANES // GROUP + group) * 8, 8), :] = jnp.sum(
                part.reshape(GROUP // 8, 8, LANES), axis=0
            )
        full_half = columns(half).reshape(LANES // 8, 8, LANES)
        product = full_half[0]
        for k in range(1, LANES // 8):
            product = product * full_half[k]
        at = pl.ds((block * LANES // STRETCH) * 8, 8)
        if (block * LANES) % STRETCH == 0:
            level[at, :] = product
        else:
            level[at, :] = level[at, :] * product
        sector = columns(sector_ref[one, :].astype(F32)).astype(jnp.int32)
        first = GLOBAL_F + sector * SECTOR_F
        mask = (ids < GLOBAL_F) | ((ids >= first) & (ids < first + SECTOR_F))
        active[rows, :] = jnp.where(mask, load_ref[rows, :].astype(F32), 0.0).astype(BF16)
        scale[rows, :] = jnp.where(mask, scale[rows, :], 0.0)

    def compute(index, slot, logits, steep):
        draw_rows = draws[unit_rows(index), :]
        lanes = pl.ds(pl.multiple_of(index * UNIT, UNIT), UNIT)
        acc = jnp.zeros((8, UNIT), F32)
        product = None
        for r in range(0, OBL, ROWS):
            rows = pl.ds(r, ROWS)
            score = lax.dot_general(active[rows, :], draw_rows, NT, preferred_element_type=F32)
            arg = score * wide(inverse[rows, :]) + wide(offset[rows, :])
            if logits:
                denom = lax.erf(arg) + wide(shift[rows, :])
                share = pltpu.reciprocal(denom)
                if not steep:
                    kept[slot, rows, :] = share
            else:
                share = kept[slot, rows, :]
            if steep:
                slopes[rows, lanes] = (jnp.exp2((arg * arg) * -LOG2_E) * share * share).astype(BF16)
            if not logits:
                continue
            loss = share * wide(gain[rows, :])
            if r % STRETCH == 0:
                product = denom[:8]
            for k in range(0 if r % STRETCH else 1, ROWS // 8):
                product = product * denom[k * 8 : k * 8 + 8]
            for g in range(0, ROWS, GROUP):
                some = loss[g : g + 8]
                for k in range(1, GROUP // 8):
                    some = some + loss[g + k * 8 : g + k * 8 + 8]
                acc = acc + (some - wide(centre[pl.ds((r + g) // GROUP * 8, 8), :]))
            if (r + ROWS) % STRETCH == 0:
                acc = acc + jnp.log(product * wide(level[pl.ds(r // STRETCH * 8, 8), :]))
        if logits:
            logit[pl.ds(index, 1), :] = jnp.sum(acc, axis=0, keepdims=True)

    for step in range(1, DEPTH):
        copy1(step, rem(z + DEPTH - step, DEPTH)).wait_recv()
    for step in (1, 3, 2):
        copy2(step, 0).start()

    def swap(i):
        return i + 1 + rem(i, 2) - div(i, 2)

    def order(n):
        early = swap(jnp.minimum(div(jnp.maximum(n - 1, 0), 2), 2))
        odd = rem(n, 2)
        late = jnp.maximum(n - 6, 0)
        g, i = div(late, 3), rem(late, 3)
        before = jnp.where(g == 0, 0, swap(jnp.maximum(g - 1, 0)))
        d = jnp.where(n < 6, jnp.where((n > 0) & (odd == 0), early, 0), jnp.where((i == 2) | (g == 3), 2, 1 + 2 * i))
        e = jnp.where(n < 6, jnp.where(odd == 1, early, 0), jnp.where((i == 2) | (g == 3), before, swap(jnp.minimum(g, 2))))
        return d, e

    def unit_of(k):
        mine = (k == 0) | (k == 2) | ((rem(k, 2) == 1) & (k > 2) & (k < UNITS - 1))
        n = jnp.where(mine, div(k + 1, 2), jnp.where(k == UNITS - 1, UNITS // 2 - 1, div(k, 2) - (k > 1)))
        d, e = order(n)
        return mine, d, e, jnp.where(mine, own_index(d, e), partner_index(d, e))

    def arrive(k):
        mine, d, e, index = unit_of(k)

        @pl.when(mine)
        def _():
            @pl.when((d == 0) & (e > 0))
            def _():
                copy2(e, e).wait_recv()

            direct = (d == 1) | (d == 3) | ((d == 2) & (e == LAST))

            @pl.when(direct)
            def _():
                copy3(e, d, d).wait_recv()

            @pl.when((d == 2) & (e != LAST))
            def _():
                for half in range(2):
                    relayed(e, half).wait_recv()

            @pl.when(d == 0)
            def _():
                for step in (1, 3):
                    copy3(e, step, 0).start()

            forward(d, e, own_index(d, e)).start()

            @pl.when((d == 0) & (e == LAST))
            def _():
                copy3(e, 2, 0).start()

            for half in range(2):

                @pl.when((d == 1 + 2 * half) & (e != LAST))
                def _():
                    relay(e, half).start()

        @pl.when(jnp.logical_not(mine))
        def _():
            forward(d, e, partner_index(d, e)).wait_recv()

        return index

    def turn(steep, pair, carry):
        first, second = arrive(2 * pair), arrive(2 * pair + 1)
        compute(first, 2 * pair - FULL, True, steep)
        compute(second, 2 * pair + 1 - FULL, True, steep)
        return carry

    lax.fori_loop(0, FULL // 2, functools.partial(turn, True), 0)
    lax.fori_loop(FULL // 2, UNITS // 2, functools.partial(turn, False), 0)

    def late_slopes(part):
        def two(pair, carry):
            indices = [unit_of(2 * pair + i)[3] for i in range(2)]
            for i in range(2):
                compute(indices[i], 2 * pair + i - FULL, False, True)
            return carry

        third = (UNITS - FULL) // 6
        lax.fori_loop(FULL // 2 + part * third, FULL // 2 + (part + 1) * third, two, 0)

    def tile(j):
        return (
            pl.ds(pl.multiple_of(div(j, SIDE) * 8, 8), 8),
            pl.ds(pl.multiple_of(rem(j, SIDE) * LANES, LANES), LANES),
        )

    def reduce1(step, j, peer):
        return pltpu.make_async_remote_copy(
            src_ref=logit.at[tile(j)],
            dst_ref=part1.at[plane],
            send_sem=send_r.at[0, step],
            recv_sem=recv_r.at[0, step],
            device_id=peer,
            device_id_type=MESH,
        )

    def reduce2(step, peer):
        return pltpu.make_async_remote_copy(
            src_ref=part2.at[stack],
            dst_ref=part2.at[stack],
            send_sem=send_r.at[1, step],
            recv_sem=recv_r.at[1, step],
            device_id=peer,
            device_id_type=MESH,
        )

    def reduce3(step, peer):
        return pltpu.make_async_remote_copy(
            src_ref=total.at[tile(plane)],
            dst_ref=total.at[tile(plane)],
            send_sem=send_r.at[2, step],
            recv_sem=recv_r.at[2, step],
            device_id=peer,
            device_id_type=MESH,
        )

    def arrival1(step):
        j = plane_from(step)
        return pltpu.make_async_remote_copy(
            src_ref=logit.at[tile(plane)],
            dst_ref=part1.at[j],
            send_sem=send_r.at[0, step],
            recv_sem=recv_r.at[0, step],
            device_id=plane_peer(j),
            device_id_type=MESH,
        )

    def arrival2(step):
        j = stack_from(step)
        return pltpu.make_async_remote_copy(
            src_ref=part2.at[stack],
            dst_ref=part2.at[j],
            send_sem=send_r.at[1, step],
            recv_sem=recv_r.at[1, step],
            device_id=stack_peer(j),
            device_id_type=MESH,
        )

    def arrival3(step):
        j = plane_from(step)
        return pltpu.make_async_remote_copy(
            src_ref=total.at[tile(plane)],
            dst_ref=total.at[tile(j)],
            send_sem=send_r.at[2, step],
            recv_sem=recv_r.at[2, step],
            device_id=plane_peer(j),
            device_id_type=MESH,
        )

    def to_plane(step):
        j = plane_to(step)
        return reduce1(step, j, plane_peer(j))

    def to_stack(step):
        return reduce2(step, stack_peer(stack_to(step)))

    def back_to_plane(step):
        return reduce3(step, plane_peer(plane_to(step)))

    for step in FAR_PLANE:
        to_plane(step).start()
    part1[plane] = logit[tile(plane)]
    late_slopes(0)
    for step in range(1, PEERS):
        arrival1(step).wait_recv()
    part2[stack] = jnp.sum(part1[...], axis=0)
    for step in FAR_STACK:
        to_stack(step).start()
    late_slopes(1)
    for step in range(1, PEERS):
        arrival2(step).wait_recv()
    total[tile(plane)] = jnp.sum(part2[...], axis=0)
    for step in FAR_PLANE:
        back_to_plane(step).start()
    late_slopes(2)
    for step in range(1, DEPTH):
        copy1(step, z).wait_send()
    for step in range(1, SIDE):
        copy2(step, 0).wait_send()
        for e in range(SIDE):
            if step != 2 or e == LAST:
                copy3(e, step, 0).wait_send()
    for e in range(SIDE):
        for half in range(2):
            if e != LAST:
                relay(e, half).wait_send()
    for d in range(SIDE):
        for e in range(SIDE):
            forward(d, e, own_index(d, e)).wait_send()
    for step in range(1, PEERS):
        to_plane(step).wait_send()
        to_stack(step).wait_send()
    for step in range(1, PEERS):
        arrival3(step).wait_recv()
    for step in range(1, PEERS):
        back_to_plane(step).wait_send()

    logits = total[...]
    raw = jnp.exp(logits - jnp.max(logits))
    norm = 1.0 / jnp.sum(raw)
    total[...] = raw
    own_row = total[pl.ds(own_index(0, 0), 1), :]
    own = jnp.zeros((1, OWN), F32)
    for k in range(DEPTH):
        own = jnp.where(z == k, own_row[:, k * OWN : (k + 1) * OWN], own)
    weight_ref[...] = own * (norm * SCENARIOS)

    sens_ref[...] = jnp.zeros_like(sens_ref)

    def add(n, carry):
        at = pl.ds(pl.multiple_of(n * DEEP, DEEP), DEEP)
        rows = [total[pl.ds(n * (DEEP // UNIT) + k, 1), :] for k in range(DEEP // UNIT)]
        row = jnp.broadcast_to(jnp.concatenate(rows, axis=1), (16, DEEP)).astype(BF16)
        weighted = slopes[:, at] * jnp.concatenate([row] * (OBL // 16), axis=0)
        sens_ref[...] += jnp.dot(weighted, draws[at, :], preferred_element_type=F32)
        return carry

    lax.fori_loop(0, SCENARIOS // DEEP, add, 0)
    sens_ref[...] = sens_ref[...] * (scale[...] * norm)


def shards(factor_draws, loadings, sector, threshold, idio, exposure, theta):
    rows = OBL // LANES
    vmem = pl.BlockSpec(memory_space=pltpu.VMEM)
    constant = pltpu.VMEM((OBL, LANES), F32)
    dma = pltpu.SemaphoreType.DMA
    weights, sensitivities = pl.pallas_call(
        kernel,
        out_shape=[
            jax.ShapeDtypeStruct((1, OWN), F32),
            jax.ShapeDtypeStruct((OBL, FACTORS), F32),
        ],
        in_specs=[pl.BlockSpec(memory_space=pl.ANY)] * 6 + [pl.BlockSpec(memory_space=pltpu.SMEM)],
        out_specs=[vmem] * 2,
        scratch_shapes=[
            pltpu.VMEM((OBL, FACTORS), BF16),
            pltpu.VMEM((rows, LANES), jnp.int32),
            pltpu.VMEM((rows, LANES), BF16),
            pltpu.VMEM((rows, LANES), BF16),
            pltpu.VMEM((rows, LANES), BF16),
            dma((6,)),
            pltpu.VMEM((SCENARIOS, FACTORS), BF16),
            pltpu.VMEM((OBL, SCENARIOS), BF16),
            pltpu.VMEM((UNITS - FULL, OBL, UNIT), F32),
            pltpu.VMEM((OBL, FACTORS), BF16),
            constant,
            constant,
            constant,
            constant,
            pltpu.VMEM((OBL // GROUP * 8, LANES), F32),
            pltpu.VMEM((OBL // STRETCH * 8, LANES), F32),
            constant,
            pltpu.VMEM((UNITS, UNIT), F32),
            pltpu.VMEM((UNITS, UNIT), F32),
            pltpu.VMEM((PEERS, 8, LANES), F32),
            pltpu.VMEM((PEERS, 8, LANES), F32),
            dma((DEPTH,)),
            dma((DEPTH,)),
            dma((SIDE,)),
            dma((SIDE,)),
            dma((SIDE, SIDE)),
            dma((SIDE, SIDE)),
            dma((SIDE, 2)),
            dma((SIDE, 2)),
            dma((SIDE, SIDE)),
            dma((SIDE, SIDE)),
            dma((3, PEERS)),
            dma((3, PEERS)),
        ],
        compiler_params=pltpu.CompilerParams(
            collective_id=0, has_side_effects=True, vmem_limit_bytes=58 << 20
        ),
    )(
        factor_draws,
        loadings,
        sector.reshape(rows, LANES),
        threshold.reshape(rows, LANES),
        idio.reshape(rows, LANES),
        exposure.reshape(rows, LANES),
        theta,
    )
    return weights.reshape(OWN), sensitivities


def solution(mesh):
    return jax.shard_map(
        shards,
        mesh=mesh,
        in_specs=(
            P(("scen", "obl"), None),
            P(("scen", "obl"), None),
            P(("scen", "obl")),
            P(("scen", "obl")),
            P(("scen", "obl")),
            P(("scen", "obl")),
            P(),
        ),
        out_specs=(P(("scen", "obl")), P(("scen", "obl"), None)),
        check_vma=False,
    )
```

```python
import functools

import jax
import jax.numpy as jnp
from jax import lax
from jax.experimental import pallas as pl
from jax.experimental.pallas import tpu as pltpu
from jax.sharding import PartitionSpec as P

F32 = jnp.float32
BF16 = jnp.bfloat16
MESH = pl.DeviceIdType.MESH
LANES = 128
FACTORS = 128
GLOBAL_F = 32
SECTOR_F = 8
SIDE = 4
DEPTH = 8
OWN = 64
UNIT = DEPTH * OWN
HALF = SIDE * SIDE * UNIT
SCENARIOS = 2 * HALF
UNITS = SCENARIOS // UNIT
OBL = 512
ROWS = 128
GROUP = 64
STRETCH = 256
DEEP = 4096
FULL = 8
PEERS = SIDE * SIDE
FAR_PLANE = sorted(range(1, PEERS), key=lambda s: -min(s // SIDE, SIDE - s // SIDE) - min(s % SIDE, SIDE - s % SIDE))
FAR_STACK = sorted(range(1, PEERS), key=lambda s: -min(s // 2, DEPTH - s // 2))
ROOT_HALF = 0.7071067811865476
NORMAL_PEAK = 0.3989422804014327
SCALE_OUT = 300.0
LOG2_E = 1.4426950408889634
NT = (((1,), (1,)), ((), ()))


def div(a, b):
    return lax.div(a, jnp.int32(b))


def rem(a, b):
    return lax.rem(a, jnp.int32(b))


def place():
    scen, obl = lax.axis_index("scen"), lax.axis_index("obl")
    z = div(obl, 8) * 2 + div(scen, 4)
    return rem(div(obl, 2), 4), rem(scen, 4), z, rem(obl, 2)


def device(x, y, z, core):
    return (rem(z, 2) * 4 + y, div(z, 2) * 8 + x * 2 + core)


def columns(row):
    return jnp.transpose(jnp.broadcast_to(row, (LANES, LANES)))


def wide(value):
    return jnp.concatenate([value] * (UNIT // LANES), axis=1)


def kernel(
    draws_hbm,
    load_hbm,
    sector_hbm,
    threshold_hbm,
    idio_hbm,
    exposure_hbm,
    theta_ref,
    weight_ref,
    sens_ref,
    load_ref,
    sector_ref,
    threshold_ref,
    idio_ref,
    exposure_ref,
    local,
    draws,
    slopes,
    kept,
    active,
    inverse,
    offset,
    shift,
    gain,
    centre,
    level,
    scale,
    logit,
    total,
    part1,
    part2,
    send1,
    recv1,
    send2,
    recv2,
    send3,
    recv3,
    send_f,
    recv_f,
    send_r,
    recv_r,
):
    x, y, z, core = place()
    p1 = y + core * (x - y)
    p2 = x + core * (y - x)

    def along1(step):
        q = rem(p1 + step, SIDE)
        return device(x + core * (q - x), y + (1 - core) * (q - y), z, core)

    def along2(step):
        q = rem(p2 + step, SIDE)
        return device(x + (1 - core) * (q - x), y + core * (q - y), z, core)

    partner = device(x, y, z, 1 - core)
    plane = x * SIDE + y
    stack = z * 2 + core

    def plane_to(step):
        return rem(x + step // SIDE, SIDE) * SIDE + rem(y + step % SIDE, SIDE)

    def plane_from(step):
        return plane_to((SIDE - step // SIDE) % SIDE * SIDE + (SIDE - step % SIDE) % SIDE)

    def stack_to(step):
        return rem(z + step // 2, DEPTH) * 2 + rem(core + step % 2, 2)

    def stack_from(step):
        return stack_to((DEPTH - step // 2) % DEPTH * 2 + step % 2)

    def plane_peer(j):
        return device(div(j, SIDE), rem(j, SIDE), z, core)

    def stack_peer(j):
        return device(x, y, div(j, 2), rem(j, 2))

    def fetch(source, target, slot):
        copy = pltpu.make_async_copy(source, target, local.at[slot])
        copy.start()
        return copy

    inputs = [
        fetch(sector_hbm, sector_ref, 0),
        fetch(threshold_hbm, threshold_ref, 1),
        fetch(idio_hbm, idio_ref, 2),
        fetch(exposure_hbm, exposure_ref, 3),
        fetch(load_hbm, load_ref, 4),
    ]

    barrier = pltpu.get_barrier_semaphore()
    for step in range(1, PEERS):
        for peer in (plane_peer(plane_to(step)), stack_peer(stack_to(step))):
            pl.semaphore_signal(barrier, inc=1, device_id=peer, device_id_type=MESH)

    def unit_index(half, a, b):
        return half * PEERS + a * SIDE + b

    def unit_rows(index):
        return pl.ds(pl.multiple_of(index * UNIT, UNIT), UNIT)

    def own_index(d, e):
        return unit_index(core, rem(p2 + SIDE - d, SIDE), rem(p1 + SIDE - e, SIDE))

    def partner_index(d, e):
        return unit_index(1 - core, rem(p1 + SIDE - d, SIDE), rem(p2 + SIDE - e, SIDE))

    def copy1(step, from_z):
        rows = pl.ds(pl.multiple_of(own_index(0, 0) * UNIT + from_z * OWN, OWN), OWN)
        return pltpu.make_async_remote_copy(
            src_ref=draws.at[rows],
            dst_ref=draws.at[rows],
            send_sem=send1.at[step],
            recv_sem=recv1.at[step],
            device_id=device(x, y, rem(z + step, DEPTH), core),
            device_id_type=MESH,
        )

    def unit_copy(index, send, recv, peer):
        rows = unit_rows(index)
        return pltpu.make_async_remote_copy(
            src_ref=draws.at[rows],
            dst_ref=draws.at[rows],
            send_sem=send,
            recv_sem=recv,
            device_id=peer,
            device_id_type=MESH,
        )

    def copy2(step, e):
        return unit_copy(own_index(0, e), send2.at[step], recv2.at[step], along1(step))

    def copy3(e, step, d):
        return unit_copy(own_index(d, e), send3.at[e, step], recv3.at[e, step], along2(step))

    def forward(d, e, index):
        return unit_copy(index, send_f.at[d, e], recv_f.at[d, e], partner)

    mine = pl.ds(pl.multiple_of(own_index(0, 0) * UNIT + z * OWN, OWN), OWN)
    own_draws = fetch(draws_hbm, draws.at[mine], 5)
    own_draws.wait()
    pl.semaphore_wait(barrier, 2 * (PEERS - 1))
    for step in (4, 3, 5, 2, 6, 1, 7):
        copy1(step, z).start()

    for copy in inputs:
        copy.wait()

    twist = theta_ref[0]
    ids = lax.broadcasted_iota(jnp.int32, (LANES, FACTORS), 1)
    for block in range(OBL // LANES):
        rows = pl.ds(block * LANES, LANES)
        one = pl.ds(block, 1)
        idio = idio_ref[one, :].astype(F32)
        amount = exposure_ref[one, :].astype(F32)
        limit = threshold_ref[one, :].astype(F32)
        growth = jnp.exp(twist * amount)
        half = 0.5 * (growth - 1.0)
        spread = ROOT_HALF / idio
        costs = twist * amount * growth / (growth - 1.0)
        inverse[rows, :] = columns(spread)
        offset[rows, :] = columns(limit * spread)
        shift[rows, :] = columns(1.0 / half + 1.0)
        gain[rows, :] = columns(costs / half)
        scale[rows, :] = columns(
            (SCALE_OUT * NORMAL_PEAK) * amount * growth / (idio * half * half)
        )
        full_cost = columns(costs)
        for group in range(LANES // GROUP):
            part = full_cost[group * GROUP : (group + 1) * GROUP]
            centre[pl.ds((block * LANES // GROUP + group) * 8, 8), :] = jnp.sum(
                part.reshape(GROUP // 8, 8, LANES), axis=0
            )
        full_half = columns(half).reshape(LANES // 8, 8, LANES)
        product = full_half[0]
        for k in range(1, LANES // 8):
            product = product * full_half[k]
        at = pl.ds((block * LANES // STRETCH) * 8, 8)
        if (block * LANES) % STRETCH == 0:
            level[at, :] = product
        else:
            level[at, :] = level[at, :] * product
        sector = columns(sector_ref[one, :].astype(F32)).astype(jnp.int32)
        first = GLOBAL_F + sector * SECTOR_F
        mask = (ids < GLOBAL_F) | ((ids >= first) & (ids < first + SECTOR_F))
        active[rows, :] = jnp.where(mask, load_ref[rows, :].astype(F32), 0.0).astype(BF16)
        scale[rows, :] = jnp.where(mask, scale[rows, :], 0.0)

    def compute(index, slot, logits, steep):
        draw_rows = draws[unit_rows(index), :]
        lanes = pl.ds(pl.multiple_of(index * UNIT, UNIT), UNIT)
        acc = jnp.zeros((8, UNIT), F32)
        product = None
        for r in range(0, OBL, ROWS):
            rows = pl.ds(r, ROWS)
            score = lax.dot_general(active[rows, :], draw_rows, NT, preferred_element_type=F32)
            arg = score * wide(inverse[rows, :]) + wide(offset[rows, :])
            if logits:
                denom = lax.erf(arg) + wide(shift[rows, :])
                share = pltpu.reciprocal(denom)
                if not steep:
                    kept[slot, rows, :] = share
            else:
                share = kept[slot, rows, :]
            if steep:
                slopes[rows, lanes] = (jnp.exp2((arg * arg) * -LOG2_E) * share * share).astype(BF16)
            if not logits:
                continue
            loss = share * wide(gain[rows, :])
            if r % STRETCH == 0:
                product = denom[:8]
            for k in range(0 if r % STRETCH else 1, ROWS // 8):
                product = product * denom[k * 8 : k * 8 + 8]
            for g in range(0, ROWS, GROUP):
                some = loss[g : g + 8]
                for k in range(1, GROUP // 8):
                    some = some + loss[g + k * 8 : g + k * 8 + 8]
                acc = acc + (some - wide(centre[pl.ds((r + g) // GROUP * 8, 8), :]))
            if (r + ROWS) % STRETCH == 0:
                acc = acc + jnp.log(product * wide(level[pl.ds(r // STRETCH * 8, 8), :]))
        if logits:
            logit[pl.ds(index, 1), :] = jnp.sum(acc, axis=0, keepdims=True)

    for step in range(1, DEPTH):
        copy1(step, rem(z + DEPTH - step, DEPTH)).wait_recv()
    for step in (1, 3, 2):
        copy2(step, 0).start()

    def swap(i):
        return i + 1 + rem(i, 2) - div(i, 2)

    def order(n):
        early = swap(jnp.minimum(div(jnp.maximum(n - 1, 0), 2), 2))
        odd = jnp.where(n == 5, 0, rem(n, 2))
        late = jnp.maximum(n - 6, 0)
        g, i = div(late, 3), rem(late, 3)
        before = jnp.where(g == 0, 0, swap(jnp.maximum(g - 1, 0)))
        d = jnp.where(n < 6, jnp.where(odd == 1, early, 0), jnp.where((i == 2) | (g == 3), 2, 1 + 2 * i))
        e = jnp.where(n < 6, jnp.where((n > 0) & (odd == 0), early, 0), jnp.where((i == 2) | (g == 3), before, swap(jnp.minimum(g, 2))))
        return d, e

    def unit_of(k):
        mine = (k == 0) | (k == 2) | ((rem(k, 2) == 1) & (k > 2) & (k < UNITS - 1))
        n = jnp.where(mine, div(k + 1, 2), jnp.where(k == UNITS - 1, UNITS // 2 - 1, div(k, 2) - (k > 1)))
        d, e = order(n)
        return mine, d, e, jnp.where(mine, own_index(d, e), partner_index(d, e))

    def arrive(k):
        mine, d, e, index = unit_of(k)

        @pl.when(mine)
        def _():
            @pl.when((d == 0) & (e > 0))
            def _():
                copy2(e, e).wait_recv()

            @pl.when(d > 0)
            def _():
                copy3(e, d, d).wait_recv()

            @pl.when(d == 0)
            def _():
                for step in (1, 3):
                    copy3(e, step, 0).start()

            forward(d, e, own_index(d, e)).start()

            @pl.when(d == 0)
            def _():
                copy3(e, 2, 0).start()

        @pl.when(jnp.logical_not(mine))
        def _():
            forward(d, e, partner_index(d, e)).wait_recv()

        return index

    def turn(steep, pair, carry):
        first, second = arrive(2 * pair), arrive(2 * pair + 1)
        compute(first, 2 * pair - FULL, True, steep)
        compute(second, 2 * pair + 1 - FULL, True, steep)
        return carry

    lax.fori_loop(0, FULL // 2, functools.partial(turn, True), 0)
    lax.fori_loop(FULL // 2, UNITS // 2, functools.partial(turn, False), 0)

    def late_slopes(part):
        def two(pair, carry):
            indices = [unit_of(2 * pair + i)[3] for i in range(2)]
            for i in range(2):
                compute(indices[i], 2 * pair + i - FULL, False, True)
            return carry

        third = (UNITS - FULL) // 6
        lax.fori_loop(FULL // 2 + part * third, FULL // 2 + (part + 1) * third, two, 0)

    def tile(j):
        return (
            pl.ds(pl.multiple_of(div(j, SIDE) * 8, 8), 8),
            pl.ds(pl.multiple_of(rem(j, SIDE) * LANES, LANES), LANES),
        )

    def reduce1(step, j, peer):
        return pltpu.make_async_remote_copy(
            src_ref=logit.at[tile(j)],
            dst_ref=part1.at[plane],
            send_sem=send_r.at[0, step],
            recv_sem=recv_r.at[0, step],
            device_id=peer,
            device_id_type=MESH,
        )

    def reduce2(step, peer):
        return pltpu.make_async_remote_copy(
            src_ref=part2.at[stack],
            dst_ref=part2.at[stack],
            send_sem=send_r.at[1, step],
            recv_sem=recv_r.at[1, step],
            device_id=peer,
            device_id_type=MESH,
        )

    def reduce3(step, peer):
        return pltpu.make_async_remote_copy(
            src_ref=total.at[tile(plane)],
            dst_ref=total.at[tile(plane)],
            send_sem=send_r.at[2, step],
            recv_sem=recv_r.at[2, step],
            device_id=peer,
            device_id_type=MESH,
        )

    def arrival1(step):
        j = plane_from(step)
        return pltpu.make_async_remote_copy(
            src_ref=logit.at[tile(plane)],
            dst_ref=part1.at[j],
            send_sem=send_r.at[0, step],
            recv_sem=recv_r.at[0, step],
            device_id=plane_peer(j),
            device_id_type=MESH,
        )

    def arrival2(step):
        j = stack_from(step)
        return pltpu.make_async_remote_copy(
            src_ref=part2.at[stack],
            dst_ref=part2.at[j],
            send_sem=send_r.at[1, step],
            recv_sem=recv_r.at[1, step],
            device_id=stack_peer(j),
            device_id_type=MESH,
        )

    def arrival3(step):
        j = plane_from(step)
        return pltpu.make_async_remote_copy(
            src_ref=total.at[tile(plane)],
            dst_ref=total.at[tile(j)],
            send_sem=send_r.at[2, step],
            recv_sem=recv_r.at[2, step],
            device_id=plane_peer(j),
            device_id_type=MESH,
        )

    def to_plane(step):
        j = plane_to(step)
        return reduce1(step, j, plane_peer(j))

    def to_stack(step):
        return reduce2(step, stack_peer(stack_to(step)))

    def back_to_plane(step):
        return reduce3(step, plane_peer(plane_to(step)))

    for step in FAR_PLANE:
        to_plane(step).start()
    part1[plane] = logit[tile(plane)]
    late_slopes(0)
    for step in range(1, PEERS):
        arrival1(step).wait_recv()
    part2[stack] = jnp.sum(part1[...], axis=0)
    for step in FAR_STACK:
        to_stack(step).start()
    late_slopes(1)
    for step in range(1, PEERS):
        arrival2(step).wait_recv()
    total[tile(plane)] = jnp.sum(part2[...], axis=0)
    for step in FAR_PLANE:
        back_to_plane(step).start()
    late_slopes(2)
    for step in range(1, DEPTH):
        copy1(step, z).wait_send()
    for step in range(1, SIDE):
        copy2(step, 0).wait_send()
        for e in range(SIDE):
            copy3(e, step, 0).wait_send()
    for d in range(SIDE):
        for e in range(SIDE):
            forward(d, e, own_index(d, e)).wait_send()
    for step in range(1, PEERS):
        to_plane(step).wait_send()
        to_stack(step).wait_send()
    for step in range(1, PEERS):
        arrival3(step).wait_recv()
    for step in range(1, PEERS):
        back_to_plane(step).wait_send()

    logits = total[...]
    raw = jnp.exp(logits - jnp.max(logits))
    norm = 1.0 / jnp.sum(raw)
    total[...] = raw
    own_row = total[pl.ds(own_index(0, 0), 1), :]
    own = jnp.zeros((1, OWN), F32)
    for k in range(DEPTH):
        own = jnp.where(z == k, own_row[:, k * OWN : (k + 1) * OWN], own)
    weight_ref[...] = own * (norm * SCENARIOS)

    sens_ref[...] = jnp.zeros_like(sens_ref)

    def add(n, carry):
        at = pl.ds(pl.multiple_of(n * DEEP, DEEP), DEEP)
        rows = [total[pl.ds(n * (DEEP // UNIT) + k, 1), :] for k in range(DEEP // UNIT)]
        row = jnp.broadcast_to(jnp.concatenate(rows, axis=1), (16, DEEP)).astype(BF16)
        weighted = slopes[:, at] * jnp.concatenate([row] * (OBL // 16), axis=0)
        sens_ref[...] += jnp.dot(weighted, draws[at, :], preferred_element_type=F32)
        return carry

    lax.fori_loop(0, SCENARIOS // DEEP, add, 0)
    sens_ref[...] = sens_ref[...] * (scale[...] * norm)


def shards(factor_draws, loadings, sector, threshold, idio, exposure, theta):
    rows = OBL // LANES
    vmem = pl.BlockSpec(memory_space=pltpu.VMEM)
    constant = pltpu.VMEM((OBL, LANES), F32)
    dma = pltpu.SemaphoreType.DMA
    weights, sensitivities = pl.pallas_call(
        kernel,
        out_shape=[
            jax.ShapeDtypeStruct((1, OWN), F32),
            jax.ShapeDtypeStruct((OBL, FACTORS), F32),
        ],
        in_specs=[pl.BlockSpec(memory_space=pl.ANY)] * 6 + [pl.BlockSpec(memory_space=pltpu.SMEM)],
        out_specs=[vmem] * 2,
        scratch_shapes=[
            pltpu.VMEM((OBL, FACTORS), BF16),
            pltpu.VMEM((rows, LANES), jnp.int32),
            pltpu.VMEM((rows, LANES), BF16),
            pltpu.VMEM((rows, LANES), BF16),
            pltpu.VMEM((rows, LANES), BF16),
            dma((6,)),
            pltpu.VMEM((SCENARIOS, FACTORS), BF16),
            pltpu.VMEM((OBL, SCENARIOS), BF16),
            pltpu.VMEM((UNITS - FULL, OBL, UNIT), F32),
            pltpu.VMEM((OBL, FACTORS), BF16),
            constant,
            constant,
            constant,
            constant,
            pltpu.VMEM((OBL // GROUP * 8, LANES), F32),
            pltpu.VMEM((OBL // STRETCH * 8, LANES), F32),
            constant,
            pltpu.VMEM((UNITS, UNIT), F32),
            pltpu.VMEM((UNITS, UNIT), F32),
            pltpu.VMEM((PEERS, 8, LANES), F32),
            pltpu.VMEM((PEERS, 8, LANES), F32),
            dma((DEPTH,)),
            dma((DEPTH,)),
            dma((SIDE,)),
            dma((SIDE,)),
            dma((SIDE, SIDE)),
            dma((SIDE, SIDE)),
            dma((SIDE, SIDE)),
            dma((SIDE, SIDE)),
            dma((3, PEERS)),
            dma((3, PEERS)),
        ],
        compiler_params=pltpu.CompilerParams(
            collective_id=0, has_side_effects=True, vmem_limit_bytes=58 << 20
        ),
    )(
        factor_draws,
        loadings,
        sector.reshape(rows, LANES),
        threshold.reshape(rows, LANES),
        idio.reshape(rows, LANES),
        exposure.reshape(rows, LANES),
        theta,
    )
    return weights.reshape(OWN), sensitivities


def solution(mesh):
    return jax.shard_map(
        shards,
        mesh=mesh,
        in_specs=(
            P(("scen", "obl"), None),
            P(("scen", "obl"), None),
            P(("scen", "obl")),
            P(("scen", "obl")),
            P(("scen", "obl")),
            P(("scen", "obl")),
            P(),
        ),
        out_specs=(P(("scen", "obl")), P(("scen", "obl"), None)),
        check_vma=False,
    )
```
